256 devices in a mesh: clip: 8 (over x, z_lo), fp: 32 (over y, z_hi, core).
Axes of the slice: x: 4, y: 4, z: 8 (z_hi: 4, z_lo: 2; z = z_hi * 2 + z_lo), core: 2. Of those that a mesh axis runs over, the one named last changes fastest.
Arguments:
- tokens: bfloat16 [8, 64, 128, 768], P('clip', 'fp'), may hold values from -6 to 6
- block_cotangent: bfloat16 [8, 64, 128, 768], P('clip', 'fp'), may hold values from -6 to 6
- time_qkv: bfloat16 [768, 2304], replicated, may hold values from -8 to 8
- time_out: bfloat16 [768, 768], replicated, may hold values from -0.21875 to 0.21875
- space_qkv: bfloat16 [768, 2304], replicated, may hold values from -8 to 8
- space_out: bfloat16 [768, 768], replicated, may hold values from -0.21875 to 0.21875
Outputs:
- block_out: bfloat16 [8, 64, 128, 768], P('clip', 'fp')
- tokens_grad: bfloat16 [8, 64, 128, 768], P('clip', 'fp')
- time_qkv_grad: float32 [768, 2304], P('fp')
- time_out_grad: float32 [768, 768], P('fp')
- space_qkv_grad: float32 [768, 2304], P('fp')
- space_out_grad: float32 [768, 768], P('fp')
The draws below stay inside these ranges and needn't reach their ends.
All inputs are finite; a program needn't handle non-finite values.
Results may differ from the reference program's by a relative error of at most 0.029.
Values may be sent and summed in bfloat16 or wider, within the bound.
No kernel may reach another device: no remote copies, remote signals or barrier semaphores. Data moves between devices by JAX's collectives and lax.ppermute only.
A program may use at most 128 MiB of HBM per device.

```python
import math
import jax
import jax.numpy as jnp
from jax import lax

D = 768
HEADS = 12
HEAD = 64
F = 64
P_SIZE = 128
BATCH = 8


def head_matrix(key):
    base_part = jnp.clip(jax.random.normal(key, (D, 3, HEADS, HEAD), jnp.float32), -4.0, 4.0) / math.sqrt(D)
    key_part = jnp.clip(base_part[:, 1], -8.0, 8.0)
    stacked = jnp.stack([base_part[:, 0], key_part, base_part[:, 2]], axis=1)
    return stacked.reshape(D, 3 * D)


def draw_time_qkv(key, part):
    key = jax.random.fold_in(key, 11)
    return head_matrix(key).astype(jnp.bfloat16)


def draw_space_qkv(key, part):
    key = jax.random.fold_in(key, 23)
    return head_matrix(key).astype(jnp.bfloat16)


def level_of(key, extent, pieces, low, high):
    gain, own = 1.0, jax.random.fold_in(key, 6)
    for position, shards_of in pieces:
        steps = jnp.exp(jax.random.uniform(jax.random.fold_in(own, position), (shards_of,), jnp.float32, low / len(pieces), high / len(pieces)))
        gain = gain * jnp.repeat(steps, extent[position] // shards_of).reshape([-1 if axis == position else 1 for axis in range(len(extent))])
    return gain


def scatter_about(stream_key, extent, width, most, shards=(), held_as=jnp.bfloat16):
    drawn = width * jax.random.normal(stream_key, extent, jnp.float32)
    if shards:
        drawn = drawn * level_of(stream_key, extent, shards, -0.22, 0.18)
    return jnp.clip(drawn, -most, most).astype(held_as)


def setup_inputs(seed: int = 0) -> dict:
    keys = jax.random.split(jax.random.key(seed), 7)
    return {
        "tokens": scatter_about(keys[0], (BATCH, F, P_SIZE, D), 1.0, 6.0, ((0, 8), (1, 32))),
        "block_cotangent": scatter_about(keys[1], (BATCH, F, P_SIZE, D), 1.0, 6.0, ((0, 8), (1, 32))),
        "time_qkv": draw_time_qkv(jax.random.fold_in(keys[6], 71), 0),
        "time_out": scatter_about(keys[3], (D, D), D ** -0.5, 0.21875),
        "space_qkv": draw_space_qkv(jax.random.fold_in(keys[6], 71), 0),
        "space_out": scatter_about(keys[5], (D, D), D ** -0.5, 0.21875),
    }


TIME_SPECS = ('cqphe,ckphe->cphqk', 'cphqk,ckphe->cqphe', 'cphqk,cqphe->ckphe')
SPACE_SPECS = ('cfqhe,cfkhe->cfhqk', 'cfhqk,cfkhe->cfqhe', 'cfhqk,cfqhe->cfkhe')
EPSILON = 1e-06

def product(formula, lhs_rows, rhs_rows):
    return jnp.einsum(formula, lhs_rows.astype(jnp.float32), rhs_rows.astype(jnp.float32))

def project(matrix_rows, weight):
    flat_rows = matrix_rows.reshape(-1, matrix_rows.shape[-1])
    result = jnp.dot(flat_rows, weight, preferred_element_type=jnp.float32)
    return result.reshape(matrix_rows.shape[:-1] + (weight.shape[1],))

def project_back(matrix_rows, weight):
    flat_rows = matrix_rows.reshape(-1, matrix_rows.shape[-1])
    result = lax.dot_general(flat_rows, weight, (((1,), (1,)), ((), ())), preferred_element_type=jnp.float32)
    return result.reshape(matrix_rows.shape[:-1] + (weight.shape[0],))

def weight_grad(inputs, cotangent):
    lhs_rows = inputs.reshape(-1, inputs.shape[-1])
    rhs_rows = cotangent.reshape(-1, cotangent.shape[-1])
    return lax.dot_general(lhs_rows, rhs_rows, (((0,), (0,)), ((), ())), preferred_element_type=jnp.float32)

def normalize(values):
    widened = values.astype(jnp.float32)
    centred = widened - lax.optimization_barrier(jnp.mean(widened, axis=-1, keepdims=True))
    inverse = lax.rsqrt(lax.optimization_barrier(jnp.mean(centred * centred, axis=-1, keepdims=True)) + EPSILON)
    return (centred * inverse, inverse)

def normalize_back(normed, inverse, grad_normed):
    first_mean = lax.optimization_barrier(jnp.mean(grad_normed, axis=-1, keepdims=True))
    second_mean = lax.optimization_barrier(jnp.mean(grad_normed * normed, axis=-1, keepdims=True))
    return inverse * (grad_normed - first_mean - normed * second_mean)

def split_heads(packed):
    leading = packed.shape[:-1]
    model_width = packed.shape[-1] // 3
    heads_view = packed.reshape(leading + (3, model_width // HEAD, HEAD))
    return (heads_view[..., 0, :, :], heads_view[..., 1, :, :], heads_view[..., 2, :, :])

def attend(packed, formulas):
    queries, key_heads, value_heads = split_heads(packed)
    scores = product(formulas[0], queries, key_heads) * HEAD ** (-0.5)
    probabilities = jax.nn.softmax(scores, axis=-1)
    weights = probabilities.astype(jnp.bfloat16)
    mixture = product(formulas[1], weights, value_heads).astype(jnp.bfloat16)
    return (mixture.reshape(packed.shape[:-1] + (packed.shape[-1] // 3,)), probabilities, weights)

def attend_back(packed, probabilities, weights, grad_mixture, formulas):
    queries, key_heads, value_heads = split_heads(packed)
    grad_heads = grad_mixture.reshape(value_heads.shape)
    grad_probs = product(formulas[0], grad_heads, value_heads)
    centred = grad_probs - lax.optimization_barrier(jnp.sum(grad_probs * probabilities, axis=-1, keepdims=True))
    grad_scores = (probabilities * centred * HEAD ** (-0.5)).astype(jnp.bfloat16)
    grad_queries = product(formulas[1], grad_scores, key_heads)
    grad_keys = product(formulas[2], grad_scores, queries)
    grad_values = product(formulas[2], weights, grad_heads)
    stacked = jnp.stack([grad_queries, grad_keys, grad_values], axis=-3)
    return stacked.reshape(packed.shape).astype(jnp.bfloat16)

def sublayer(stream, qkv_weight, out_weight, formulas):
    normed, inverse = normalize(stream)
    normed_low = normed.astype(jnp.bfloat16)
    packed = project(normed_low, qkv_weight).astype(jnp.bfloat16)
    mixture, probabilities, weights = attend(packed, formulas)
    result = (stream.astype(jnp.float32) + project(mixture, out_weight)).astype(jnp.bfloat16)
    return (result, (normed, inverse, normed_low, packed, probabilities, weights, mixture))

def sublayer_back(grad_result, saved, qkv_weight, out_weight, formulas):
    normed, inverse, normed_low, packed, probabilities, weights, mixture = saved
    out_weight_grad = weight_grad(mixture, grad_result)
    grad_mixture = project_back(grad_result, out_weight).astype(jnp.bfloat16)
    grad_packed = attend_back(packed, probabilities, weights, grad_mixture, formulas)
    qkv_weight_grad = weight_grad(normed_low, grad_packed)
    grad_normed = project_back(grad_packed, qkv_weight)
    grad_stream = grad_result.astype(jnp.float32) + normalize_back(normed, inverse, grad_normed)
    return (grad_stream.astype(jnp.bfloat16), qkv_weight_grad, out_weight_grad)

def reference(tokens, block_cotangent, time_qkv, time_out, space_qkv, space_out):

    def one_clip(clip_pair):
        clip_tokens = clip_pair[0][None]
        clip_cotangent = clip_pair[1][None]
        middle, time_saved = sublayer(clip_tokens, time_qkv, time_out, TIME_SPECS)
        block_result, space_saved = sublayer(middle, space_qkv, space_out, SPACE_SPECS)
        grad_middle, space_qkv_part, space_out_part = sublayer_back(clip_cotangent, space_saved, space_qkv, space_out, SPACE_SPECS)
        grad_tokens, time_qkv_part, time_out_part = sublayer_back(grad_middle, time_saved, time_qkv, time_out, TIME_SPECS)
        return (block_result[0], grad_tokens[0], time_qkv_part, time_out_part, space_qkv_part, space_out_part)
    results = lax.map(one_clip, (tokens, block_cotangent))
    return (results[0], results[1], lax.optimization_barrier(jnp.sum(results[2], axis=0)), lax.optimization_barrier(jnp.sum(results[3], axis=0)), lax.optimization_barrier(jnp.sum(results[4], axis=0)), lax.optimization_barrier(jnp.sum(results[5], axis=0)))
```

```python
import functools

import jax
import jax.numpy as jnp
from jax import lax
from jax.experimental import pallas as pl
from jax.experimental.pallas import tpu as pltpu
from jax.sharding import Mesh, PartitionSpec as P

D = 768
HEAD = 64
PAIR = 2 * HEAD
PAIRS = D // PAIR
T = 256
ROWS = 24
HALF = D // 2
EPSILON = 1e-06
SCALE = HEAD ** (-0.5)
BF = jnp.bfloat16
F32 = jnp.float32

FP = ("y", "zh", "c")
CLIP = ("x", "zl")

NN = (((1,), (0,)), ((), ()))
NT = (((1,), (1,)), ((), ()))
TN = (((0,), (0,)), ((), ()))


def dot(a, b, dims=NN):
    return lax.dot_general(a, b, dims, preferred_element_type=F32)


def normalize(x):
    centred = x - jnp.mean(x, axis=-1, keepdims=True)
    inverse = lax.rsqrt(jnp.mean(centred * centred, axis=-1, keepdims=True) + EPSILON)
    return centred * inverse, inverse


def normalize_back(normed, inverse, grad):
    first = jnp.mean(grad, axis=-1, keepdims=True)
    second = jnp.mean(grad * normed, axis=-1, keepdims=True)
    return inverse * (grad - first - normed * second)


def iota(shape, dim):
    return lax.broadcasted_iota(jnp.int32, shape, dim)


def order(to_sent):
    sent = iota((T, T), 0 if to_sent else 1)
    natural = iota((T, T), 1 if to_sent else 0)
    source = ((sent // 4) % 2) * 128 + (sent // 8) * 4 + sent % 4
    return jnp.where(source == natural, 1.0, 0.0).astype(BF)


def chosen_rows(core):
    row = iota((HALF, D), 0)
    feature = (row // ROWS) * (2 * ROWS) + core * ROWS + row % ROWS
    return jnp.where(iota((HALF, D), 1) == feature, 1.0, 0.0).astype(BF)


def lanes(rows):
    low = iota((rows, PAIR), 1) < HEAD
    zero = jnp.zeros((rows, PAIR), BF)
    return lambda a, odd: jnp.where(low, zero, a) if odd else jnp.where(low, a, zero)


def same_patch():
    return (iota((T, T), 0) % 4) == (iota((T, T), 1) % 4)


def permute_kernel(to_sent, x_ref, o_ref):
    o_ref[...] = dot(order(to_sent), x_ref[...]).astype(BF)


def time_forward_kernel(core_ref, x_ref, wq_ref, wo_ref, middle_ref, qkv_ref, own_ref, send_ref, mixed_ref):
    x = x_ref[...].astype(F32)
    normed, _ = normalize(x)
    normed = normed.astype(BF)
    for i in range(9):
        cols = slice(i * 256, (i + 1) * 256)
        qkv_ref[:, cols] = dot(normed, wq_ref[:, cols]).astype(BF)
    keep = lanes(T)
    near = same_patch()
    for p in range(PAIRS):
        q = qkv_ref[:, p * PAIR:(p + 1) * PAIR]
        k = qkv_ref[:, D + p * PAIR:D + (p + 1) * PAIR]
        v = qkv_ref[:, 2 * D + p * PAIR:2 * D + (p + 1) * PAIR]
        weights = []
        values = []
        for odd in (False, True):
            s = dot(keep(q, odd), k, NT)
            s = jnp.where(near, s, -1e30)
            e = jnp.exp((s - jnp.max(s, axis=1, keepdims=True)) * SCALE)
            weights.append((e / jnp.sum(e, axis=1, keepdims=True)).astype(BF))
            values.append(keep(v, odd))
        mixed = dot(jnp.concatenate(weights, axis=1), jnp.concatenate(values, axis=0))
        mixed_ref[:, p * PAIR:(p + 1) * PAIR] = mixed.astype(BF)
    mixed = mixed_ref[...]
    middle_ref[...] = (x + dot(mixed, wo_ref[...])).astype(BF)
    core = core_ref[0]
    for ref, which in ((own_ref, core), (send_ref, 1 - core)):
        pick = chosen_rows(which)
        ref[0] = dot(pick, normed, NT).astype(BF)
        ref[1] = dot(pick, mixed, NT).astype(BF)


def probs_back(q, k, v, g, near):
    s = dot(k, q, NT)
    if near is not None:
        s = jnp.where(near, s, -1e30)
    e = jnp.exp((s - jnp.max(s, axis=0, keepdims=True)) * SCALE)
    probs = e / jnp.sum(e, axis=0, keepdims=True)
    dprobs = dot(v, g, NT)
    delta = jnp.sum(dprobs * probs, axis=0, keepdims=True)
    return probs.astype(BF), (probs * (dprobs - delta) * SCALE).astype(BF)


def attend_back(qkv_ref, g_ref, dqkv_ref, mixed_ref, near, blocks):
    size = T // blocks
    keep = lanes(size)
    for p in range(PAIRS):
        for b in range(blocks):
            rows = slice(b * size, (b + 1) * size)
            at = [slice(i * D + p * PAIR, i * D + (p + 1) * PAIR) for i in range(3)]
            q, k, v = (qkv_ref[rows, at[i]] for i in range(3))
            g = g_ref[rows, at[0]]
            qs, ks, vs, gs, ws, ds = [], [], [], [], [], []
            for odd in (False, True):
                q1, k1, v1, g1 = (keep(a, odd) for a in (q, k, v, g))
                w, d = probs_back(q, k1, v1, g, near)
                for into, a in ((qs, q1), (ks, k1), (vs, v1), (gs, g1), (ws, w), (ds, d)):
                    into.append(a)
            qs, ks, vs, gs = (jnp.concatenate(a, axis=0) for a in (qs, ks, vs, gs))
            dqkv_ref[rows, at[1]] = dot(jnp.concatenate(ds, axis=1), qs).astype(BF)
            dqkv_ref[rows, at[2]] = dot(jnp.concatenate(ws, axis=1), gs).astype(BF)
            dqkv_ref[rows, at[0]] = dot(jnp.concatenate(ds, axis=0), ks, TN).astype(BF)
            if mixed_ref is not None:
                mixed_ref[rows, at[0]] = dot(jnp.concatenate(ws, axis=0), vs, TN).astype(BF)


def space_kernel(
    core_ref, m_ref, cot_ref, wq_ref, wo_ref,
    out_ref, grad_ref, dqkv_ref, own_ref, send_ref,
    x_ref, qkv_ref, g_ref, mixed_ref,
):
    x_ref[...] = dot(order(False), m_ref[...]).astype(BF)
    normed, inverse = normalize(x_ref[...].astype(F32))
    low = normed.astype(BF)
    for i in range(9):
        cols = slice(i * 256, (i + 1) * 256)
        qkv_ref[:, cols] = dot(low, wq_ref[:, cols]).astype(BF)
    cot = cot_ref[...]
    g_ref[...] = dot(cot, wo_ref[...], NT).astype(BF)
    attend_back(qkv_ref, g_ref, dqkv_ref, mixed_ref, None, 2)
    grad = dot(dqkv_ref[...], wq_ref[...], NT)
    grad = cot.astype(F32) + normalize_back(normed, inverse, grad)
    grad_ref[...] = dot(order(True), grad.astype(BF)).astype(BF)
    mixed = mixed_ref[...]
    out_ref[...] = (x_ref[...].astype(F32) + dot(mixed, wo_ref[...])).astype(BF)
    core = core_ref[0]
    for ref, which in ((own_ref, core), (send_ref, 1 - core)):
        pick = chosen_rows(which)
        ref[0] = dot(pick, low, NT).astype(BF)
        ref[1] = dot(pick, mixed, NT).astype(BF)


def time_backward_kernel(x_ref, gm_ref, qkv_ref, wq_ref, wo_ref, grad_ref, dqkv_ref, g_ref):
    gm = gm_ref[...]
    g_ref[...] = dot(gm, wo_ref[...], NT).astype(BF)
    attend_back(qkv_ref, g_ref, dqkv_ref, None, same_patch(), 1)
    normed, inverse = normalize(x_ref[...].astype(F32))
    grad = dot(dqkv_ref[...], wq_ref[...], NT)
    grad_ref[...] = (gm.astype(F32) + normalize_back(normed, inverse, grad)).astype(BF)


def weights_kernel(l_ref, l2_ref, d_ref, d2_ref, g_ref, g2_ref, o_ref):
    for which in range(2):
        left = jnp.concatenate([l_ref[which], l2_ref[which]], axis=1)
        a, b = ((d_ref, d2_ref), (g_ref, g2_ref))[which]
        for j in range(a.shape[1] // HALF):
            cols = slice(j * HALF, (j + 1) * HALF)
            right = jnp.concatenate([a[:, cols], b[:, cols]], axis=0)
            o_ref[which * 6 + j] = dot(left, right).astype(BF)


def sds(*shape):
    return jax.ShapeDtypeStruct(shape, BF)


SMEM = pl.BlockSpec(memory_space=pltpu.SMEM)
VMEM = pl.BlockSpec(memory_space=pltpu.VMEM)


def call(kernel, outs, args, flops, scratch=(), name=None):
    moved = sum(a.size * a.dtype.itemsize for a in args) + 2 * sum(o.size for o in outs)
    return pl.pallas_call(
        kernel,
        out_shape=outs,
        in_specs=[SMEM if a.dtype == jnp.int32 else VMEM for a in args],
        out_specs=[VMEM] * len(outs),
        scratch_shapes=scratch,
        compiler_params=pltpu.CompilerParams(vmem_limit_bytes=48 * 2**20),
        cost_estimate=pl.CostEstimate(flops=flops, bytes_accessed=moved, transcendentals=0),
        name=name,
    )(*args)


PROJ = 2 * T * D * 3 * D
OUTP = 2 * T * D * D


def permuted(x, to_sent):
    return call(functools.partial(permute_kernel, to_sent), [sds(T, D)], [x], 2 * T * T * D)[0]


def a2a(x, axes):
    return lax.all_to_all(x, axes, 0, 0, tiled=True)


def swap(x):
    return lax.ppermute(x, "c", [(0, 1), (1, 0)])


def first_stage(left_own, left_other, d, d2, g, g2):
    partial = call(weights_kernel, [sds(8, HALF, HALF)], [left_own, left_other, d, d2, g, g2], 2 * 512 * HALF * 4 * D)[0]
    got = a2a(partial.reshape(32, HALF // 4, HALF), ("x", "zl", "y"))
    return jnp.sum(got.astype(F32), axis=0).astype(BF)


def last_stages(parts):
    both = jnp.concatenate(parts, axis=1).reshape(4, ROWS, D)
    share = jnp.sum(a2a(both, ("zh",)).astype(F32), axis=0).astype(BF)
    got = a2a(jnp.broadcast_to(share[None], (8, ROWS, D)), CLIP)
    got = got.reshape(8, ROWS, 2, HALF).transpose(2, 1, 0, 3).reshape(2, ROWS, 4 * D).astype(F32)
    return [got[0, :, :3 * D], got[0, :, 3 * D:], got[1, :, :3 * D], got[1, :, 3 * D:]]


def on_device(tokens, block_cotangent, time_qkv, time_out, space_qkv, space_out):
    core = lax.axis_index("c").astype(jnp.int32).reshape(1)
    cot = block_cotangent.reshape(T, D)
    cot_other = swap(cot)
    x = a2a(permuted(tokens.reshape(T, D), True), FP)
    middle, t_qkv, t_own, t_send = call(
        time_forward_kernel,
        [sds(T, D), sds(T, 3 * D), sds(2, HALF, T), sds(2, HALF, T)],
        [core, x, time_qkv, time_out],
        PROJ + OUTP, [pltpu.VMEM((T, D), BF)],
    )
    middle = a2a(middle, FP)
    t_other = swap(t_send)
    block_out, grad_middle, s_dqkv, s_own, s_send = call(
        space_kernel,
        [sds(T, D), sds(T, D), sds(T, 3 * D), sds(2, HALF, T), sds(2, HALF, T)],
        [core, middle, cot, space_qkv, space_out],
        2 * (PROJ + OUTP),
        [pltpu.VMEM((T, D), BF), pltpu.VMEM((T, 3 * D), BF), pltpu.VMEM((T, D), BF), pltpu.VMEM((T, D), BF)],
    )
    grad_middle = a2a(grad_middle, FP)
    space_part = first_stage(s_own, swap(s_send), s_dqkv, swap(s_dqkv), cot, cot_other)
    grad_middle_other = swap(grad_middle)
    grad_tokens, t_dqkv = call(
        time_backward_kernel,
        [sds(T, D), sds(T, 3 * D)],
        [x, grad_middle, t_qkv, time_qkv, time_out],
        PROJ + OUTP, [pltpu.VMEM((T, D), BF)],
    )
    time_part = first_stage(t_own, t_other, t_dqkv, swap(t_dqkv), grad_middle, grad_middle_other)
    tokens_grad = permuted(a2a(grad_tokens, FP), False)
    sums = last_stages([time_part, space_part])
    shape = tokens.shape
    return (block_out.reshape(shape), tokens_grad.reshape(shape), *sums)


def solution(mesh):
    fine = Mesh(mesh.devices.reshape(4, 2, 4, 4, 2), ("x", "zl", "y", "zh", "c"))
    activations = P(CLIP, FP, None, None)
    return jax.shard_map(
        on_device,
        mesh=fine,
        in_specs=(activations, activations, P(), P(), P(), P()),
        out_specs=(activations, activations, P(FP, None), P(FP, None), P(FP, None), P(FP, None)),
        check_vma=False,
    )
```

```python
import functools

import jax
import jax.numpy as jnp
from jax import lax
from jax.experimental import pallas as pl
from jax.experimental.pallas import tpu as pltpu
from jax.sharding import Mesh, PartitionSpec as P

D = 768
HEAD = 64
PAIR = 2 * HEAD
PAIRS = D // PAIR
T = 256
ROWS = 24
HALF = D // 2
BLOCK = 4 * ROWS
WHOLE = 60
QKV = 3 * D // 4
OUT = D // 4
EPSILON = 1e-06
SCALE = HEAD ** (-0.5)
BF = jnp.bfloat16
F32 = jnp.float32

FP = ("y", "zh", "c")
CLIP = ("x", "zl")

NN = (((1,), (0,)), ((), ()))
NT = (((1,), (1,)), ((), ()))
TN = (((0,), (0,)), ((), ()))


def dot(a, b, dims=NN):
    return lax.dot_general(a, b, dims, preferred_element_type=F32)


def normalize(x):
    centred = x - jnp.mean(x, axis=-1, keepdims=True)
    inverse = lax.rsqrt(jnp.mean(centred * centred, axis=-1, keepdims=True) + EPSILON)
    return centred * inverse, inverse


def normalize_back(normed, inverse, grad):
    first = jnp.mean(grad, axis=-1, keepdims=True)
    second = jnp.mean(grad * normed, axis=-1, keepdims=True)
    return inverse * (grad - first - normed * second)


def iota(shape, dim):
    return lax.broadcasted_iota(jnp.int32, shape, dim)


def order(to_sent):
    sent = iota((T, T), 0 if to_sent else 1)
    natural = iota((T, T), 1 if to_sent else 0)
    source = ((sent // 4) % 2) * 128 + (sent // 8) * 4 + sent % 4
    return jnp.where(source == natural, 1.0, 0.0).astype(BF)


def chosen_rows(core):
    row = iota((HALF, D), 0)
    feature = (row // ROWS) * (2 * ROWS) + core * ROWS + row % ROWS
    return jnp.where(iota((HALF, D), 1) == feature, 1.0, 0.0).astype(BF)


def lanes(rows):
    low = iota((rows, PAIR), 1) < HEAD
    zero = jnp.zeros((rows, PAIR), BF)
    return lambda a, odd: jnp.where(low, zero, a) if odd else jnp.where(low, a, zero)


def same_patch():
    return (iota((T, T), 0) % 4) == (iota((T, T), 1) % 4)


def permute_kernel(to_sent, x_ref, o_ref):
    o_ref[...] = dot(order(to_sent), x_ref[...]).astype(BF)


def factors_kernel(pos_ref, low_ref, mixed_ref, own_ref, send_ref):
    for ref, which in ((own_ref, pos_ref[1]), (send_ref, 1 - pos_ref[1])):
        pick = chosen_rows(which)
        ref[0] = dot(pick, low_ref[...], NT).astype(BF)
        ref[1] = dot(pick, mixed_ref[...], NT).astype(BF)


def time_forward_kernel(x_ref, wq_ref, wo_ref, middle_ref, qkv_ref, low_ref, mixed_ref):
    x = x_ref[...].astype(F32)
    normed, _ = normalize(x)
    low = normed.astype(BF)
    low_ref[...] = low
    for i in range(9):
        cols = slice(i * 256, (i + 1) * 256)
        qkv_ref[:, cols] = dot(low, wq_ref[:, cols]).astype(BF)
    keep = lanes(T)
    near = same_patch()
    for p in range(PAIRS):
        q, k, v = (qkv_ref[:, i * D + p * PAIR:i * D + (p + 1) * PAIR] for i in range(3))
        weights = []
        values = []
        for odd in (False, True):
            s = dot(keep(q, odd), k, NT)
            s = jnp.where(near, s, -1e30)
            e = jnp.exp((s - jnp.max(s, axis=1, keepdims=True)) * SCALE)
            weights.append((e / jnp.sum(e, axis=1, keepdims=True)).astype(BF))
            values.append(keep(v, odd))
        mixed = dot(jnp.concatenate(weights, axis=1), jnp.concatenate(values, axis=0))
        mixed_ref[:, p * PAIR:(p + 1) * PAIR] = mixed.astype(BF)
    middle_ref[...] = (x + dot(mixed_ref[...], wo_ref[...])).astype(BF)


def probs_back(q, k, v, g, near):
    s = dot(k, q, NT)
    if near is not None:
        s = jnp.where(near, s, -1e30)
    e = jnp.exp((s - jnp.max(s, axis=0, keepdims=True)) * SCALE)
    probs = e / jnp.sum(e, axis=0, keepdims=True)
    dprobs = dot(v, g, NT)
    delta = jnp.sum(dprobs * probs, axis=0, keepdims=True)
    return probs.astype(BF), (probs * (dprobs - delta) * SCALE).astype(BF)


def attend_back(qkv_ref, g_ref, dqkv_ref, mixed_ref, near, blocks):
    size = T // blocks
    keep = lanes(size)
    for p in range(PAIRS):
        for b in range(blocks):
            rows = slice(b * size, (b + 1) * size)
            at = [slice(i * D + p * PAIR, i * D + (p + 1) * PAIR) for i in range(3)]
            q, k, v = (qkv_ref[rows, at[i]] for i in range(3))
            g = g_ref[rows, at[0]]
            qs, ks, vs, gs, ws, ds = [], [], [], [], [], []
            for odd in (False, True):
                q1, k1, v1, g1 = (keep(a, odd) for a in (q, k, v, g))
                w, d = probs_back(q, k1, v1, g, near)
                for into, a in ((qs, q1), (ks, k1), (vs, v1), (gs, g1), (ws, w), (ds, d)):
                    into.append(a)
            qs, ks, vs, gs = (jnp.concatenate(a, axis=0) for a in (qs, ks, vs, gs))
            dqkv_ref[rows, at[1]] = dot(jnp.concatenate(ds, axis=1), qs).astype(BF)
            dqkv_ref[rows, at[2]] = dot(jnp.concatenate(ws, axis=1), gs).astype(BF)
            dqkv_ref[rows, at[0]] = dot(jnp.concatenate(ds, axis=0), ks, TN).astype(BF)
            if mixed_ref is not None:
                mixed_ref[rows, at[0]] = dot(jnp.concatenate(ws, axis=0), vs, TN).astype(BF)


def space_kernel(m_ref, cot_ref, wq_ref, wo_ref, grad_ref, dqkv_ref, x_ref, low_ref, mixed_ref, qkv_ref, g_ref):
    x_ref[...] = dot(order(False), m_ref[...]).astype(BF)
    normed, inverse = normalize(x_ref[...].astype(F32))
    low = normed.astype(BF)
    low_ref[...] = low
    for i in range(9):
        cols = slice(i * 256, (i + 1) * 256)
        qkv_ref[:, cols] = dot(low, wq_ref[:, cols]).astype(BF)
    cot = cot_ref[...]
    g_ref[...] = dot(cot, wo_ref[...], NT).astype(BF)
    attend_back(qkv_ref, g_ref, dqkv_ref, mixed_ref, None, 2)
    grad = dot(dqkv_ref[...], wq_ref[...], NT)
    grad = cot.astype(F32) + normalize_back(normed, inverse, grad)
    grad_ref[...] = dot(order(True), grad.astype(BF)).astype(BF)


def space_out_kernel(x_ref, mixed_ref, wo_ref, out_ref):
    out_ref[...] = (x_ref[...].astype(F32) + dot(mixed_ref[...], wo_ref[...])).astype(BF)


def turned(pos, k):
    return (pos + k) % 4


def turned(pos, k):
    return (pos + k) % 4


def time_attend_kernel(gm_ref, qkv_ref, wo_ref, dqkv_ref, g_ref):
    g_ref[...] = dot(gm_ref[...], wo_ref[...], NT).astype(BF)
    attend_back(qkv_ref, g_ref, dqkv_ref, None, same_patch(), 1)


def time_grad_kernel(x_ref, gm_ref, dqkv_ref, wq_ref, grad_ref):
    normed, inverse = normalize(x_ref[...].astype(F32))
    grad = dot(dqkv_ref[...], wq_ref[...], NT)
    grad_ref[...] = (gm_ref[...].astype(F32) + normalize_back(normed, inverse, grad)).astype(BF)


def weights_kernel(pos_ref, l_ref, l2_ref, d_ref, d2_ref, g_ref, g2_ref, o_ref):
    over_x = pos_ref[1] == 0
    for a_ref, b_ref, which, at, width in ((g_ref, g2_ref, 1, QKV, OUT), (d_ref, d2_ref, 0, 0, QKV)):
        left = jnp.concatenate([l_ref[which], l2_ref[which]], axis=1)
        part = dot(left, jnp.concatenate([a_ref[...], b_ref[...]], axis=0)).astype(BF)
        for i in range(4):
            for j in range(4):
                block = part[i * BLOCK:(i + 1) * BLOCK, j * width:(j + 1) * width]
                o_ref[jnp.where(over_x, j, i), jnp.where(over_x, i, j), :, at:at + width] = block


def add(refs):
    total = refs[0][...].astype(F32)
    for ref in refs[1:]:
        total += ref[...].astype(F32)
    return total.astype(BF)


def add_first(ref):
    total = ref[0].astype(F32)
    for i in range(1, ref.shape[0]):
        total += ref[i].astype(F32)
    return total.astype(BF)


def pieces_kernel(t_ref, s_ref, o_ref):
    for i in range(4):
        o_ref[i, :, :D] = add([t_ref.at[k, i] for k in range(4)])
        o_ref[i, :, D:] = add([s_ref.at[k, i] for k in range(4)])


def first_sum_kernel(got_ref, o_ref):
    o_ref[...] = add_first(got_ref)


def pair_sum_kernel(own_ref, other_ref, o_ref):
    o_ref[...] = add([own_ref, other_ref])


def spread_kernel(pos_ref, *refs):
    outs, held_ref = refs[4:8], refs[8]
    for k in range(4):
        held_ref[turned(pos_ref[0], 4 - k)] = refs[k][...].astype(F32)
    for i in range(2):
        for j in range(4):
            outs[2 * i][:, j * QKV:(j + 1) * QKV] = held_ref[j, :, i * D:i * D + QKV]
            outs[2 * i + 1][:, j * OUT:(j + 1) * OUT] = held_ref[j, :, i * D + QKV:(i + 1) * D]


def sds(*shape, dtype=BF):
    return jax.ShapeDtypeStruct(shape, dtype)


SMEM = pl.BlockSpec(memory_space=pltpu.SMEM)
VMEM = pl.BlockSpec(memory_space=pltpu.VMEM)


def call(kernel, outs, args, flops, scratch=(), mib=48):
    moved = sum(a.size * a.dtype.itemsize for a in (*args, *outs))
    return pl.pallas_call(
        kernel,
        out_shape=outs,
        in_specs=[SMEM if a.dtype == jnp.int32 else VMEM for a in args],
        out_specs=[VMEM] * len(outs),
        scratch_shapes=scratch,
        compiler_params=pltpu.CompilerParams(vmem_limit_bytes=mib * 2**20),
        cost_estimate=pl.CostEstimate(flops=flops, bytes_accessed=moved if flops else 0, transcendentals=0),
    )(*args)


PROJ = 2 * T * D * 3 * D
OUTP = 2 * T * D * D


def permuted(x, to_sent):
    return call(functools.partial(permute_kernel, to_sent), [sds(T, D)], [x], 2 * T * T * D)[0]


def a2a(x, axes):
    return lax.all_to_all(x, axes, 0, 0, tiled=True)


def factors(pos, low, mixed):
    return call(
        factors_kernel, [sds(2, HALF, T)] * 2, [pos, low, mixed], 2 * OUTP, mib=WHOLE
    )


def weights(*factors):
    return call(weights_kernel, [sds(4, 4, BLOCK, D)], factors, 2 * 512 * HALF * 4 * D, mib=WHOLE)[0]


def crossed(x, first):
    device = [[[(i * 4 + j) * 2 + core for core in range(2)] for j in range(4)] for i in range(4)]
    along_x = [[device[i][j][1 - first] for i in range(4)] for j in range(4)]
    along_y = [[device[i][j][first] for j in range(4)] for i in range(4)]
    return lax.all_to_all(x, ("x", "y", "c"), 0, 0, tiled=True, axis_index_groups=along_x + along_y)


def swap(x):
    return lax.ppermute(x, "c", [(0, 1), (1, 0)])


def shifted(x, axis, k):
    return lax.ppermute(x, axis, [(i, (i + k) % 4) for i in range(4)])


def exchange(pieces, axis):
    return [pieces[0]] + [shifted(pieces[k], axis, k) for k in (1, 2, 3)]


def after(*arrays):
    return lax.optimization_barrier(arrays)


def on_device(tokens, block_cotangent, time_qkv, time_out, space_qkv, space_out):
    pos = jnp.stack([lax.axis_index(axis).astype(jnp.int32) for axis in ("x", "c")])
    cot = block_cotangent.reshape(T, D)
    x = a2a(permuted(tokens.reshape(T, D), True), FP)
    x, cot_other = after(x, swap(cot))
    middle, t_qkv, t_low, t_mixed = call(
        time_forward_kernel,
        [sds(T, D), sds(T, 3 * D), sds(T, D), sds(T, D)],
        [x, time_qkv, time_out],
        PROJ + OUTP, mib=WHOLE,
    )
    middle = a2a(middle, FP)
    t_own, t_send = factors(pos, t_low, t_mixed)
    middle, t_other = after(middle, swap(t_send))
    grad_middle, s_dqkv, natural, s_low, s_mixed = call(
        space_kernel,
        [sds(T, D), sds(T, 3 * D), sds(T, D), sds(T, D), sds(T, D)],
        [middle, cot, space_qkv, space_out],
        2 * (PROJ + OUTP),
        [pltpu.VMEM((T, 3 * D), BF), pltpu.VMEM((T, D), BF)], mib=WHOLE,
    )
    grad_middle = a2a(grad_middle, FP)
    s_own, s_send = factors(pos, s_low, s_mixed)
    space = weights(pos, s_own, swap(s_send), s_dqkv, swap(s_dqkv), cot, cot_other)
    block_out = call(space_out_kernel, [sds(T, D)], [natural, s_mixed, space_out], OUTP, mib=WHOLE)[0]
    grad_middle, block_out, space = after(grad_middle, block_out, space)
    space = crossed(space, 1)
    t_dqkv = call(
        time_attend_kernel, [sds(T, 3 * D)], [grad_middle, t_qkv, time_out], PROJ + OUTP, [pltpu.VMEM((T, D), BF)]
    )[0]
    grad_tokens = call(time_grad_kernel, [sds(T, D)], [x, grad_middle, t_dqkv, time_qkv], PROJ)[0]
    time = weights(pos, t_own, t_other, t_dqkv, swap(t_dqkv), grad_middle, swap(grad_middle))
    time, grad_tokens = after(time, grad_tokens)
    time = crossed(time, 1)
    got = crossed(call(pieces_kernel, [sds(4, BLOCK, 2 * D)], [time, space], 0)[0], 0)
    got = call(first_sum_kernel, [sds(BLOCK, 2 * D)], [got], 0)[0]
    got = a2a(got.reshape(4, ROWS, 2 * D), ("zh",))
    got, grad_tokens = after(got, grad_tokens)
    tokens_grad = permuted(a2a(grad_tokens, FP), False)
    share = call(first_sum_kernel, [sds(ROWS, 2 * D)], [got], 0)[0]
    other = lax.ppermute(share, "zl", [(0, 1), (1, 0)])
    share = call(pair_sum_kernel, [sds(ROWS, 2 * D)], [share, other], 0)[0]
    sizes = [3 * D, D, 3 * D, D]
    sums = call(
        spread_kernel, [sds(ROWS, size, dtype=F32) for size in sizes], [pos, *exchange([share] * 4, "x")], 0,
        [pltpu.VMEM((4, ROWS, 2 * D), F32)],
    )
    shape = tokens.shape
    return (block_out.reshape(shape), tokens_grad.reshape(shape), *sums)


def solution(mesh):
    fine = Mesh(mesh.devices.reshape(4, 2, 4, 4, 2), ("x", "zl", "y", "zh", "c"))
    activations = P(CLIP, FP, None, None)
    return jax.shard_map(
        on_device,
        mesh=fine,
        in_specs=(activations, activations, P(), P(), P(), P()),
        out_specs=(activations, activations, P(FP, None), P(FP, None), P(FP, None), P(FP, None)),
        check_vma=False,
    )
```

```python
import functools

import jax
import jax.numpy as jnp
from jax import lax
from jax.experimental import pallas as pl
from jax.experimental.pallas import tpu as pltpu
from jax.sharding import Mesh, PartitionSpec as P

D = 768
HEAD = 64
PAIR = 2 * HEAD
PAIRS = D // PAIR
T = 256
ROWS = 24
HALF = D // 2
BLOCK = 4 * ROWS
WHOLE = 60
QKV = 3 * D // 4
OUT = D // 4
EPSILON = 1e-06
SCALE = HEAD ** (-0.5)
BF = jnp.bfloat16
F32 = jnp.float32

FP = ("y", "zh", "c")
CLIP = ("x", "zl")

NN = (((1,), (0,)), ((), ()))
NT = (((1,), (1,)), ((), ()))
TN = (((0,), (0,)), ((), ()))


def dot(a, b, dims=NN):
    return lax.dot_general(a, b, dims, preferred_element_type=F32)


def normalize(x):
    centred = x - jnp.mean(x, axis=-1, keepdims=True)
    inverse = lax.rsqrt(jnp.mean(centred * centred, axis=-1, keepdims=True) + EPSILON)
    return centred * inverse, inverse


def normalize_back(normed, inverse, grad):
    first = jnp.mean(grad, axis=-1, keepdims=True)
    second = jnp.mean(grad * normed, axis=-1, keepdims=True)
    return inverse * (grad - first - normed * second)


def iota(shape, dim):
    return lax.broadcasted_iota(jnp.int32, shape, dim)


def order(to_sent):
    sent = iota((T, T), 0 if to_sent else 1)
    natural = iota((T, T), 1 if to_sent else 0)
    source = ((sent // 4) % 2) * 128 + (sent // 8) * 4 + sent % 4
    return jnp.where(source == natural, 1.0, 0.0).astype(BF)


def chosen_rows(core):
    row = iota((HALF, D), 0)
    feature = (row // ROWS) * (2 * ROWS) + core * ROWS + row % ROWS
    return jnp.where(iota((HALF, D), 1) == feature, 1.0, 0.0).astype(BF)


def lanes(rows):
    low = iota((rows, PAIR), 1) < HEAD
    zero = jnp.zeros((rows, PAIR), BF)
    return lambda a, odd: jnp.where(low, zero, a) if odd else jnp.where(low, a, zero)


def same_patch():
    return (iota((T, T), 0) % 4) == (iota((T, T), 1) % 4)


def permute_kernel(to_sent, x_ref, o_ref):
    o_ref[...] = dot(order(to_sent), x_ref[...]).astype(BF)


def factors_kernel(pos_ref, low_ref, mixed_ref, own_ref, send_ref):
    for ref, which in ((own_ref, pos_ref[1]), (send_ref, 1 - pos_ref[1])):
        pick = chosen_rows(which)
        ref[0] = dot(pick, low_ref[...], NT).astype(BF)
        ref[1] = dot(pick, mixed_ref[...], NT).astype(BF)


def time_forward_kernel(x_ref, wq_ref, wo_ref, middle_ref, qkv_ref, low_ref, mixed_ref):
    x = x_ref[...].astype(F32)
    normed, _ = normalize(x)
    low = normed.astype(BF)
    low_ref[...] = low
    for i in range(9):
        cols = slice(i * 256, (i + 1) * 256)
        qkv_ref[:, cols] = dot(low, wq_ref[:, cols]).astype(BF)
    keep = lanes(T)
    near = same_patch()
    for p in range(PAIRS):
        q, k, v = (qkv_ref[:, i * D + p * PAIR:i * D + (p + 1) * PAIR] for i in range(3))
        weights = []
        values = []
        for odd in (False, True):
            s = dot(keep(q, odd), k, NT)
            s = jnp.where(near, s, -1e30)
            e = jnp.exp((s - jnp.max(s, axis=1, keepdims=True)) * SCALE)
            weights.append((e / jnp.sum(e, axis=1, keepdims=True)).astype(BF))
            values.append(keep(v, odd))
        mixed = dot(jnp.concatenate(weights, axis=1), jnp.concatenate(values, axis=0))
        mixed_ref[:, p * PAIR:(p + 1) * PAIR] = mixed.astype(BF)
    middle_ref[...] = (x + dot(mixed_ref[...], wo_ref[...])).astype(BF)


def probs_back(q, k, v, g, near):
    s = dot(k, q, NT)
    if near is not None:
        s = jnp.where(near, s, -1e30)
    e = jnp.exp((s - jnp.max(s, axis=0, keepdims=True)) * SCALE)
    probs = e / jnp.sum(e, axis=0, keepdims=True)
    dprobs = dot(v, g, NT)
    delta = jnp.sum(dprobs * probs, axis=0, keepdims=True)
    return probs.astype(BF), (probs * (dprobs - delta) * SCALE).astype(BF)


def attend_back(qkv_ref, g_ref, dqkv_ref, mixed_ref, near, blocks):
    size = T // blocks
    keep = lanes(size)
    for p in range(PAIRS):
        for b in range(blocks):
            rows = slice(b * size, (b + 1) * size)
            at = [slice(i * D + p * PAIR, i * D + (p + 1) * PAIR) for i in range(3)]
            q, k, v = (qkv_ref[rows, at[i]] for i in range(3))
            g = g_ref[rows, at[0]]
            qs, ks, vs, gs, ws, ds = [], [], [], [], [], []
            for odd in (False, True):
                q1, k1, v1, g1 = (keep(a, odd) for a in (q, k, v, g))
                w, d = probs_back(q, k1, v1, g, near)
                for into, a in ((qs, q1), (ks, k1), (vs, v1), (gs, g1), (ws, w), (ds, d)):
                    into.append(a)
            qs, ks, vs, gs = (jnp.concatenate(a, axis=0) for a in (qs, ks, vs, gs))
            dqkv_ref[rows, at[1]] = dot(jnp.concatenate(ds, axis=1), qs).astype(BF)
            dqkv_ref[rows, at[2]] = dot(jnp.concatenate(ws, axis=1), gs).astype(BF)
            dqkv_ref[rows, at[0]] = dot(jnp.concatenate(ds, axis=0), ks, TN).astype(BF)
            if mixed_ref is not None:
                mixed_ref[rows, at[0]] = dot(jnp.concatenate(ws, axis=0), vs, TN).astype(BF)


def space_kernel(m_ref, cot_ref, wq_ref, wo_ref, grad_ref, dqkv_ref, x_ref, low_ref, mixed_ref, qkv_ref, g_ref):
    x_ref[...] = dot(order(False), m_ref[...]).astype(BF)
    normed, inverse = normalize(x_ref[...].astype(F32))
    low = normed.astype(BF)
    low_ref[...] = low
    for i in range(9):
        cols = slice(i * 256, (i + 1) * 256)
        qkv_ref[:, cols] = dot(low, wq_ref[:, cols]).astype(BF)
    cot = cot_ref[...]
    g_ref[...] = dot(cot, wo_ref[...], NT).astype(BF)
    attend_back(qkv_ref, g_ref, dqkv_ref, mixed_ref, None, 2)
    grad = dot(dqkv_ref[...], wq_ref[...], NT)
    grad = cot.astype(F32) + normalize_back(normed, inverse, grad)
    grad_ref[...] = dot(order(True), grad.astype(BF)).astype(BF)


def space_out_kernel(x_ref, mixed_ref, wo_ref, out_ref):
    out_ref[...] = (x_ref[...].astype(F32) + dot(mixed_ref[...], wo_ref[...])).astype(BF)


def turned(pos, k):
    return (pos + k) % 4


def turned(pos, k):
    return (pos + k) % 4


def time_attend_kernel(gm_ref, qkv_ref, wo_ref, dqkv_ref, g_ref):
    g_ref[...] = dot(gm_ref[...], wo_ref[...], NT).astype(BF)
    attend_back(qkv_ref, g_ref, dqkv_ref, None, same_patch(), 1)


def time_grad_kernel(x_ref, gm_ref, dqkv_ref, wq_ref, grad_ref):
    normed, inverse = normalize(x_ref[...].astype(F32))
    grad = dot(dqkv_ref[...], wq_ref[...], NT)
    grad_ref[...] = (gm_ref[...].astype(F32) + normalize_back(normed, inverse, grad)).astype(BF)


def weights_kernel(pos_ref, l_ref, l2_ref, d_ref, d2_ref, g_ref, g2_ref, o_ref):
    over_x = pos_ref[1] == 0
    for a_ref, b_ref, which, at, width in ((g_ref, g2_ref, 1, QKV, OUT), (d_ref, d2_ref, 0, 0, QKV)):
        left = jnp.concatenate([l_ref[which], l2_ref[which]], axis=1)
        part = dot(left, jnp.concatenate([a_ref[...], b_ref[...]], axis=0)).astype(BF)
        for i in range(4):
            for j in range(4):
                block = part[i * BLOCK:(i + 1) * BLOCK, j * width:(j + 1) * width]
                o_ref[jnp.where(over_x, j, i), jnp.where(over_x, i, j), :, at:at + width] = block


def weights_by_distance_kernel(pos_ref, l_ref, l2_ref, d_ref, d2_ref, g_ref, g2_ref, *refs):
    outs, held_ref = refs[:4], refs[4]
    weights_kernel(pos_ref, l_ref, l2_ref, d_ref, d2_ref, g_ref, g2_ref, held_ref)
    for k in range(4):
        outs[k][...] = held_ref[turned(pos_ref[2], k)]


def add(refs):
    total = refs[0][...].astype(F32)
    for ref in refs[1:]:
        total += ref[...].astype(F32)
    return total.astype(BF)


def add_first(ref):
    total = ref[0].astype(F32)
    for i in range(1, ref.shape[0]):
        total += ref[i].astype(F32)
    return total.astype(BF)


def first_sum_kernel(got_ref, o_ref):
    o_ref[...] = add_first(got_ref)


def pieces_kernel(s_ref, *refs):
    o_ref = refs[4]
    for i in range(4):
        o_ref[i, :, :D] = add([ref.at[i] for ref in refs[:4]])
        o_ref[i, :, D:] = add([s_ref.at[k, i] for k in range(4)])


def copies_kernel(got_ref, o_ref):
    total = add_first(got_ref)
    for i in range(8):
        o_ref[i] = total


def spread_kernel(got_ref, *outs):
    for i in range(2):
        for j in range(4):
            part = add([got_ref.at[2 * j, :, i * D:(i + 1) * D], got_ref.at[2 * j + 1, :, i * D:(i + 1) * D]]).astype(F32)
            outs[2 * i][:, j * QKV:(j + 1) * QKV] = part[:, :QKV]
            outs[2 * i + 1][:, j * OUT:(j + 1) * OUT] = part[:, QKV:]


def sds(*shape, dtype=BF):
    return jax.ShapeDtypeStruct(shape, dtype)


SMEM = pl.BlockSpec(memory_space=pltpu.SMEM)
VMEM = pl.BlockSpec(memory_space=pltpu.VMEM)


def call(kernel, outs, args, flops, scratch=(), mib=48):
    moved = sum(a.size * a.dtype.itemsize for a in (*args, *outs))
    return pl.pallas_call(
        kernel,
        out_shape=outs,
        in_specs=[SMEM if a.dtype == jnp.int32 else VMEM for a in args],
        out_specs=[VMEM] * len(outs),
        scratch_shapes=scratch,
        compiler_params=pltpu.CompilerParams(vmem_limit_bytes=mib * 2**20),
        cost_estimate=pl.CostEstimate(flops=flops, bytes_accessed=moved if flops else 0, transcendentals=0),
    )(*args)


PROJ = 2 * T * D * 3 * D
OUTP = 2 * T * D * D


def permuted(x, to_sent):
    return call(functools.partial(permute_kernel, to_sent), [sds(T, D)], [x], 2 * T * T * D)[0]


def a2a(x, axes):
    return lax.all_to_all(x, axes, 0, 0, tiled=True)


def factors(pos, low, mixed):
    return call(
        factors_kernel, [sds(2, HALF, T)] * 2, [pos, low, mixed], 2 * OUTP, mib=WHOLE
    )


def weights(*factors):
    return call(weights_kernel, [sds(4, 4, BLOCK, D)], factors, 2 * 512 * HALF * 4 * D, mib=WHOLE)[0]


def rings(first):
    device = [[[(i * 4 + j) * 2 + core for core in range(2)] for j in range(4)] for i in range(4)]
    along_x = [[device[i][j][1 - first] for i in range(4)] for j in range(4)]
    along_y = [[device[i][j][first] for j in range(4)] for i in range(4)]
    return along_x + along_y


def crossed(x, first):
    return lax.all_to_all(x, ("x", "y", "c"), 0, 0, tiled=True, axis_index_groups=rings(first))


def crossed_steps(pieces, first):
    return [pieces[0]] + [
        lax.ppermute(pieces[k], ("x", "y", "c"), [(ring[i], ring[(i + k) % 4]) for ring in rings(first) for i in range(4)])
        for k in (1, 2, 3)
    ]


def swap(x):
    return lax.ppermute(x, "c", [(0, 1), (1, 0)])


def after(*arrays):
    return lax.optimization_barrier(arrays)


def on_device(tokens, block_cotangent, time_qkv, time_out, space_qkv, space_out):
    x_at, y_at, core = (lax.axis_index(axis).astype(jnp.int32) for axis in ("x", "y", "c"))
    pos = jnp.stack([x_at, core, jnp.where(core == 0, x_at, y_at)])
    cot = block_cotangent.reshape(T, D)
    x = a2a(permuted(tokens.reshape(T, D), True), FP)
    x, cot_other = after(x, swap(cot))
    middle, t_qkv, t_low, t_mixed = call(
        time_forward_kernel,
        [sds(T, D), sds(T, 3 * D), sds(T, D), sds(T, D)],
        [x, time_qkv, time_out],
        PROJ + OUTP, mib=WHOLE,
    )
    middle = a2a(middle, FP)
    t_own, t_send = factors(pos, t_low, t_mixed)
    middle, t_other = after(middle, swap(t_send))
    grad_middle, s_dqkv, natural, s_low, s_mixed = call(
        space_kernel,
        [sds(T, D), sds(T, 3 * D), sds(T, D), sds(T, D), sds(T, D)],
        [middle, cot, space_qkv, space_out],
        2 * (PROJ + OUTP),
        [pltpu.VMEM((T, 3 * D), BF), pltpu.VMEM((T, D), BF)], mib=WHOLE,
    )
    grad_middle = a2a(grad_middle, FP)
    s_own, s_send = factors(pos, s_low, s_mixed)
    space = weights(pos, s_own, swap(s_send), s_dqkv, swap(s_dqkv), cot, cot_other)
    block_out = call(space_out_kernel, [sds(T, D)], [natural, s_mixed, space_out], OUTP, mib=WHOLE)[0]
    grad_middle, block_out, space = after(grad_middle, block_out, space)
    space = crossed(space, 1)
    t_dqkv = call(
        time_attend_kernel, [sds(T, 3 * D)], [grad_middle, t_qkv, time_out], PROJ + OUTP, [pltpu.VMEM((T, D), BF)]
    )[0]
    grad_tokens = call(time_grad_kernel, [sds(T, D)], [x, grad_middle, t_dqkv, time_qkv], PROJ)[0]
    time = call(
        weights_by_distance_kernel, [sds(4, BLOCK, D)] * 4,
        [pos, t_own, t_other, t_dqkv, swap(t_dqkv), grad_middle, swap(grad_middle)], 2 * 512 * HALF * 4 * D,
        [pltpu.VMEM((4, 4, BLOCK, D), BF)], mib=WHOLE,
    )
    grad_tokens, space, *time = after(grad_tokens, space, *time)
    tokens_grad = a2a(grad_tokens, FP)
    got = call(pieces_kernel, [sds(4, BLOCK, 2 * D)], [space, *crossed_steps(time, 1)], 0)[0]
    got, tokens_grad = after(got, tokens_grad)
    got = call(first_sum_kernel, [sds(BLOCK, 2 * D)], [crossed(got, 0)], 0)[0]
    got = a2a(got.reshape(4, ROWS, 2 * D), ("zh",))
    tokens_grad = permuted(tokens_grad, False)
    shares = call(copies_kernel, [sds(8, ROWS, 2 * D)], [got], 0)[0]
    sizes = [3 * D, D, 3 * D, D]
    sums = call(spread_kernel, [sds(ROWS, size, dtype=F32) for size in sizes], [a2a(shares, CLIP)], 0)
    shape = tokens.shape
    return (block_out.reshape(shape), tokens_grad.reshape(shape), *sums)


def solution(mesh):
    fine = Mesh(mesh.devices.reshape(4, 2, 4, 4, 2), ("x", "zl", "y", "zh", "c"))
    activations = P(CLIP, FP, None, None)
    return jax.shard_map(
        on_device,
        mesh=fine,
        in_specs=(activations, activations, P(), P(), P(), P()),
        out_specs=(activations, activations, P(FP, None), P(FP, None), P(FP, None), P(FP, None)),
        check_vma=False,
    )
```

```python
import functools

import jax
import jax.numpy as jnp
from jax import lax
from jax.experimental import pallas as pl
from jax.experimental.pallas import tpu as pltpu
from jax.sharding import Mesh, PartitionSpec as P

D = 768
HEAD = 64
PAIR = 2 * HEAD
PAIRS = D // PAIR
T = 256
ROWS = 24
HALF = D // 2
BLOCK = 4 * ROWS
WHOLE = 60
QKV = 3 * D // 4
OUT = D // 4
EPSILON = 1e-06
SCALE = HEAD ** (-0.5)
BF = jnp.bfloat16
F32 = jnp.float32

FP = ("y", "zh", "c")
CLIP = ("x", "zl")

NN = (((1,), (0,)), ((), ()))
NT = (((1,), (1,)), ((), ()))
TN = (((0,), (0,)), ((), ()))


def dot(a, b, dims=NN):
    return lax.dot_general(a, b, dims, preferred_element_type=F32)


def normalize(x):
    centred = x - jnp.mean(x, axis=-1, keepdims=True)
    inverse = lax.rsqrt(jnp.mean(centred * centred, axis=-1, keepdims=True) + EPSILON)
    return centred * inverse, inverse


def normalize_back(normed, inverse, grad):
    first = jnp.mean(grad, axis=-1, keepdims=True)
    second = jnp.mean(grad * normed, axis=-1, keepdims=True)
    return inverse * (grad - first - normed * second)


def iota(shape, dim):
    return lax.broadcasted_iota(jnp.int32, shape, dim)


def order(to_sent):
    sent = iota((T, T), 0 if to_sent else 1)
    natural = iota((T, T), 1 if to_sent else 0)
    source = ((sent // 4) % 2) * 128 + (sent // 8) * 4 + sent % 4
    return jnp.where(source == natural, 1.0, 0.0).astype(BF)


def chosen_rows(core):
    row = iota((HALF, D), 0)
    feature = (row // ROWS) * (2 * ROWS) + core * ROWS + row % ROWS
    return jnp.where(iota((HALF, D), 1) == feature, 1.0, 0.0).astype(BF)


def lanes(rows):
    low = iota((rows, PAIR), 1) < HEAD
    zero = jnp.zeros((rows, PAIR), BF)
    return lambda a, odd: jnp.where(low, zero, a) if odd else jnp.where(low, a, zero)


def same_patch():
    return (iota((T, T), 0) % 4) == (iota((T, T), 1) % 4)


def permute_kernel(to_sent, x_ref, o_ref):
    o_ref[...] = dot(order(to_sent), x_ref[...]).astype(BF)


def factors_kernel(pos_ref, low_ref, mixed_ref, own_ref, send_ref):
    for ref, which in ((own_ref, pos_ref[1]), (send_ref, 1 - pos_ref[1])):
        pick = chosen_rows(which)
        ref[0] = dot(pick, low_ref[...], NT).astype(BF)
        ref[1] = dot(pick, mixed_ref[...], NT).astype(BF)


def time_forward_kernel(x_ref, wq_ref, wo_ref, middle_ref, qkv_ref, low_ref, mixed_ref):
    x = x_ref[...].astype(F32)
    normed, _ = normalize(x)
    low = normed.astype(BF)
    low_ref[...] = low
    for i in range(9):
        cols = slice(i * 256, (i + 1) * 256)
        qkv_ref[:, cols] = dot(low, wq_ref[:, cols]).astype(BF)
    keep = lanes(T)
    near = same_patch()
    for p in range(PAIRS):
        q, k, v = (qkv_ref[:, i * D + p * PAIR:i * D + (p + 1) * PAIR] for i in range(3))
        weights = []
        values = []
        for odd in (False, True):
            s = dot(keep(q, odd), k, NT)
            s = jnp.where(near, s, -1e30)
            e = jnp.exp((s - jnp.max(s, axis=1, keepdims=True)) * SCALE)
            weights.append((e / jnp.sum(e, axis=1, keepdims=True)).astype(BF))
            values.append(keep(v, odd))
        mixed = dot(jnp.concatenate(weights, axis=1), jnp.concatenate(values, axis=0))
        mixed_ref[:, p * PAIR:(p + 1) * PAIR] = mixed.astype(BF)
    middle_ref[...] = (x + dot(mixed_ref[...], wo_ref[...])).astype(BF)


def probs_back(q, k, v, g, near):
    s = dot(k, q, NT)
    if near is not None:
        s = jnp.where(near, s, -1e30)
    e = jnp.exp((s - jnp.max(s, axis=0, keepdims=True)) * SCALE)
    probs = e / jnp.sum(e, axis=0, keepdims=True)
    dprobs = dot(v, g, NT)
    delta = jnp.sum(dprobs * probs, axis=0, keepdims=True)
    return probs.astype(BF), (probs * (dprobs - delta) * SCALE).astype(BF)


def attend_back(qkv_ref, g_ref, dqkv_ref, mixed_ref, near, blocks):
    size = T // blocks
    keep = lanes(size)
    for p in range(PAIRS):
        for b in range(blocks):
            rows = slice(b * size, (b + 1) * size)
            at = [slice(i * D + p * PAIR, i * D + (p + 1) * PAIR) for i in range(3)]
            q, k, v = (qkv_ref[rows, at[i]] for i in range(3))
            g = g_ref[rows, at[0]]
            qs, ks, vs, gs, ws, ds = [], [], [], [], [], []
            for odd in (False, True):
                q1, k1, v1, g1 = (keep(a, odd) for a in (q, k, v, g))
                w, d = probs_back(q, k1, v1, g, near)
                for into, a in ((qs, q1), (ks, k1), (vs, v1), (gs, g1), (ws, w), (ds, d)):
                    into.append(a)
            qs, ks, vs, gs = (jnp.concatenate(a, axis=0) for a in (qs, ks, vs, gs))
            dqkv_ref[rows, at[1]] = dot(jnp.concatenate(ds, axis=1), qs).astype(BF)
            dqkv_ref[rows, at[2]] = dot(jnp.concatenate(ws, axis=1), gs).astype(BF)
            dqkv_ref[rows, at[0]] = dot(jnp.concatenate(ds, axis=0), ks, TN).astype(BF)
            if mixed_ref is not None:
                mixed_ref[rows, at[0]] = dot(jnp.concatenate(ws, axis=0), vs, TN).astype(BF)


def project_back_kernel(cot_ref, wo_ref, g_ref):
    g_ref[...] = dot(cot_ref[...], wo_ref[...], NT).astype(BF)


def space_kernel(m_ref, cot_ref, g_ref, wq_ref, grad_ref, dqkv_ref, x_ref, low_ref, mixed_ref, qkv_ref):
    x_ref[...] = dot(order(False), m_ref[...]).astype(BF)
    normed, inverse = normalize(x_ref[...].astype(F32))
    low = normed.astype(BF)
    low_ref[...] = low
    for i in range(9):
        cols = slice(i * 256, (i + 1) * 256)
        qkv_ref[:, cols] = dot(low, wq_ref[:, cols]).astype(BF)
    attend_back(qkv_ref, g_ref, dqkv_ref, mixed_ref, None, 2)
    grad = dot(dqkv_ref[...], wq_ref[...], NT)
    grad = cot_ref[...].astype(F32) + normalize_back(normed, inverse, grad)
    grad_ref[...] = dot(order(True), grad.astype(BF)).astype(BF)


def space_out_kernel(x_ref, mixed_ref, wo_ref, out_ref):
    out_ref[...] = (x_ref[...].astype(F32) + dot(mixed_ref[...], wo_ref[...])).astype(BF)


def turned(pos, k):
    return (pos + k) % 4


def turned(pos, k):
    return (pos + k) % 4


def time_attend_kernel(gm_ref, qkv_ref, wo_ref, dqkv_ref, g_ref):
    g_ref[...] = dot(gm_ref[...], wo_ref[...], NT).astype(BF)
    attend_back(qkv_ref, g_ref, dqkv_ref, None, same_patch(), 1)


def time_grad_kernel(x_ref, gm_ref, dqkv_ref, wq_ref, grad_ref):
    normed, inverse = normalize(x_ref[...].astype(F32))
    grad = dot(dqkv_ref[...], wq_ref[...], NT)
    grad_ref[...] = (gm_ref[...].astype(F32) + normalize_back(normed, inverse, grad)).astype(BF)


def weights_kernel(pos_ref, l_ref, l2_ref, d_ref, d2_ref, g_ref, g2_ref, o_ref):
    over_x = pos_ref[1] == 0
    for a_ref, b_ref, which, at, width in ((g_ref, g2_ref, 1, QKV, OUT), (d_ref, d2_ref, 0, 0, QKV)):
        left = jnp.concatenate([l_ref[which], l2_ref[which]], axis=1)
        part = dot(left, jnp.concatenate([a_ref[...], b_ref[...]], axis=0)).astype(BF)
        for i in range(4):
            for j in range(4):
                block = part[i * BLOCK:(i + 1) * BLOCK, j * width:(j + 1) * width]
                o_ref[jnp.where(over_x, j, i), jnp.where(over_x, i, j), :, at:at + width] = block


def weights_by_distance_kernel(pos_ref, l_ref, l2_ref, d_ref, d2_ref, g_ref, g2_ref, *refs):
    outs, held_ref = refs[:4], refs[4]
    weights_kernel(pos_ref, l_ref, l2_ref, d_ref, d2_ref, g_ref, g2_ref, held_ref)
    for k in range(4):
        outs[k][...] = held_ref[turned(pos_ref[2], k)]


def add(refs):
    total = refs[0][...].astype(F32)
    for ref in refs[1:]:
        total += ref[...].astype(F32)
    return total.astype(BF)


def add_first(ref):
    total = ref[0].astype(F32)
    for i in range(1, ref.shape[0]):
        total += ref[i].astype(F32)
    return total.astype(BF)


def sum_kernel(*refs):
    refs[4][...] = add(refs[:4])


def pieces_kernel(pos_ref, s_ref, *refs):
    for k in range(4):
        owner = turned(pos_ref[3], k)
        refs[4 + k][:, :D] = add([ref.at[owner] for ref in refs[:4]])
        refs[4 + k][:, D:] = add([s_ref.at[i, owner] for i in range(4)])


def copies_kernel(got_ref, o_ref):
    total = add_first(got_ref)
    for i in range(8):
        o_ref[i] = total


def spread_kernel(got_ref, *outs):
    for i in range(2):
        for j in range(4):
            part = add([got_ref.at[2 * j, :, i * D:(i + 1) * D], got_ref.at[2 * j + 1, :, i * D:(i + 1) * D]]).astype(F32)
            outs[2 * i][:, j * QKV:(j + 1) * QKV] = part[:, :QKV]
            outs[2 * i + 1][:, j * OUT:(j + 1) * OUT] = part[:, QKV:]


def sds(*shape, dtype=BF):
    return jax.ShapeDtypeStruct(shape, dtype)


SMEM = pl.BlockSpec(memory_space=pltpu.SMEM)
VMEM = pl.BlockSpec(memory_space=pltpu.VMEM)


def call(kernel, outs, args, flops, scratch=(), mib=48):
    moved = sum(a.size * a.dtype.itemsize for a in (*args, *outs))
    return pl.pallas_call(
        kernel,
        out_shape=outs,
        in_specs=[SMEM if a.dtype == jnp.int32 else VMEM for a in args],
        out_specs=[VMEM] * len(outs),
        scratch_shapes=scratch,
        compiler_params=pltpu.CompilerParams(vmem_limit_bytes=mib * 2**20),
        cost_estimate=pl.CostEstimate(flops=flops, bytes_accessed=moved if flops else 0, transcendentals=0),
    )(*args)


PROJ = 2 * T * D * 3 * D
OUTP = 2 * T * D * D


def permuted(x, to_sent):
    return call(functools.partial(permute_kernel, to_sent), [sds(T, D)], [x], 2 * T * T * D)[0]


def a2a(x, axes):
    return lax.all_to_all(x, axes, 0, 0, tiled=True)


def factors(pos, low, mixed):
    return call(
        factors_kernel, [sds(2, HALF, T)] * 2, [pos, low, mixed], 2 * OUTP, mib=WHOLE
    )


def weights(*factors):
    return call(weights_kernel, [sds(4, 4, BLOCK, D)], factors, 2 * 512 * HALF * 4 * D, mib=WHOLE)[0]


def rings(first):
    device = [[[(i * 4 + j) * 2 + core for core in range(2)] for j in range(4)] for i in range(4)]
    along_x = [[device[i][j][1 - first] for i in range(4)] for j in range(4)]
    along_y = [[device[i][j][first] for j in range(4)] for i in range(4)]
    return along_x + along_y


def crossed(x, first):
    return lax.all_to_all(x, ("x", "y", "c"), 0, 0, tiled=True, axis_index_groups=rings(first))


def crossed_steps(pieces, first):
    return [pieces[0]] + [
        lax.ppermute(pieces[k], ("x", "y", "c"), [(ring[i], ring[(i + k) % 4]) for ring in rings(first) for i in range(4)])
        for k in (1, 2, 3)
    ]


def swap(x):
    return lax.ppermute(x, "c", [(0, 1), (1, 0)])


def after(*arrays):
    return lax.optimization_barrier(arrays)


def on_device(tokens, block_cotangent, time_qkv, time_out, space_qkv, space_out):
    x_at, y_at, core = (lax.axis_index(axis).astype(jnp.int32) for axis in ("x", "y", "c"))
    pos = jnp.stack([x_at, core, jnp.where(core == 0, x_at, y_at), jnp.where(core == 0, y_at, x_at)])
    cot = block_cotangent.reshape(T, D)
    x = a2a(permuted(tokens.reshape(T, D), True), FP)
    x, cot_other = after(x, swap(cot))
    middle, t_qkv, t_low, t_mixed = call(
        time_forward_kernel,
        [sds(T, D), sds(T, 3 * D), sds(T, D), sds(T, D)],
        [x, time_qkv, time_out],
        PROJ + OUTP, mib=WHOLE,
    )
    middle = a2a(middle, FP)
    t_own, t_send = factors(pos, t_low, t_mixed)
    s_dmixed = call(project_back_kernel, [sds(T, D)], [cot, space_out], OUTP, mib=WHOLE)[0]
    middle, t_other, s_dmixed = after(middle, swap(t_send), s_dmixed)
    grad_middle, s_dqkv, natural, s_low, s_mixed = call(
        space_kernel,
        [sds(T, D), sds(T, 3 * D), sds(T, D), sds(T, D), sds(T, D)],
        [middle, cot, s_dmixed, space_qkv],
        2 * PROJ,
        [pltpu.VMEM((T, 3 * D), BF)], mib=WHOLE,
    )
    grad_middle = a2a(grad_middle, FP)
    s_own, s_send = factors(pos, s_low, s_mixed)
    space = weights(pos, s_own, swap(s_send), s_dqkv, swap(s_dqkv), cot, cot_other)
    block_out = call(space_out_kernel, [sds(T, D)], [natural, s_mixed, space_out], OUTP, mib=WHOLE)[0]
    grad_middle, block_out, space = after(grad_middle, block_out, space)
    space = crossed(space, 1)
    t_dqkv = call(
        time_attend_kernel, [sds(T, 3 * D)], [grad_middle, t_qkv, time_out], PROJ + OUTP, [pltpu.VMEM((T, D), BF)]
    )[0]
    grad_tokens = call(time_grad_kernel, [sds(T, D)], [x, grad_middle, t_dqkv, time_qkv], PROJ)[0]
    time = call(
        weights_by_distance_kernel, [sds(4, BLOCK, D)] * 4,
        [pos, t_own, t_other, t_dqkv, swap(t_dqkv), grad_middle, swap(grad_middle)], 2 * 512 * HALF * 4 * D,
        [pltpu.VMEM((4, 4, BLOCK, D), BF)], mib=WHOLE,
    )
    grad_tokens, space, *time = after(grad_tokens, space, *time)
    tokens_grad = a2a(grad_tokens, FP)
    pieces = call(
        pieces_kernel, [sds(BLOCK, 2 * D)] * 4, [pos, space, *crossed_steps(time, 1)], 0,
    )
    got = call(sum_kernel, [sds(BLOCK, 2 * D)], crossed_steps(pieces, 0), 0)[0]
    got, tokens_grad = after(got, tokens_grad)
    got = a2a(got.reshape(4, ROWS, 2 * D), ("zh",))
    tokens_grad = permuted(tokens_grad, False)
    shares = call(copies_kernel, [sds(8, ROWS, 2 * D)], [got], 0)[0]
    sizes = [3 * D, D, 3 * D, D]
    sums = call(spread_kernel, [sds(ROWS, size, dtype=F32) for size in sizes], [a2a(shares, CLIP)], 0)
    shape = tokens.shape
    return (block_out.reshape(shape), tokens_grad.reshape(shape), *sums)


def solution(mesh):
    fine = Mesh(mesh.devices.reshape(4, 2, 4, 4, 2), ("x", "zl", "y", "zh", "c"))
    activations = P(CLIP, FP, None, None)
    return jax.shard_map(
        on_device,
        mesh=fine,
        in_specs=(activations, activations, P(), P(), P(), P()),
        out_specs=(activations, activations, P(FP, None), P(FP, None), P(FP, None), P(FP, None)),
        check_vma=False,
    )
```

```python
import functools

import jax
import jax.numpy as jnp
from jax import lax
from jax.experimental import pallas as pl
from jax.experimental.pallas import tpu as pltpu
from jax.sharding import Mesh, PartitionSpec as P

D = 768
HEAD = 64
PAIR = 2 * HEAD
PAIRS = D // PAIR
T = 256
ROWS = 24
HALF = D // 2
BLOCK = 4 * ROWS
WHOLE = 60
QKV = 3 * D // 4
OUT = D // 4
EPSILON = 1e-06
SCALE = HEAD ** (-0.5)
BF = jnp.bfloat16
F32 = jnp.float32

FP = ("y", "zh", "c")
CLIP = ("x", "zl")

NN = (((1,), (0,)), ((), ()))
NT = (((1,), (1,)), ((), ()))
TN = (((0,), (0,)), ((), ()))


def dot(a, b, dims=NN):
    return lax.dot_general(a, b, dims, preferred_element_type=F32)


def normalize(x):
    centred = x - jnp.mean(x, axis=-1, keepdims=True)
    inverse = lax.rsqrt(jnp.mean(centred * centred, axis=-1, keepdims=True) + EPSILON)
    return centred * inverse, inverse


def normalize_back(normed, inverse, grad):
    first = jnp.mean(grad, axis=-1, keepdims=True)
    second = jnp.mean(grad * normed, axis=-1, keepdims=True)
    return inverse * (grad - first - normed * second)


def iota(shape, dim):
    return lax.broadcasted_iota(jnp.int32, shape, dim)


def order(to_sent):
    sent = iota((T, T), 0 if to_sent else 1)
    natural = iota((T, T), 1 if to_sent else 0)
    source = ((sent // 4) % 2) * 128 + (sent // 8) * 4 + sent % 4
    return jnp.where(source == natural, 1.0, 0.0).astype(BF)


def chosen_rows(core):
    row = iota((HALF, D), 0)
    feature = (row // ROWS) * (2 * ROWS) + core * ROWS + row % ROWS
    return jnp.where(iota((HALF, D), 1) == feature, 1.0, 0.0).astype(BF)


def lanes(rows):
    low = iota((rows, PAIR), 1) < HEAD
    zero = jnp.zeros((rows, PAIR), BF)
    return lambda a, odd: jnp.where(low, zero, a) if odd else jnp.where(low, a, zero)


def same_patch():
    return (iota((T, T), 0) % 4) == (iota((T, T), 1) % 4)


def permute_kernel(to_sent, x_ref, o_ref):
    o_ref[...] = dot(order(to_sent), x_ref[...]).astype(BF)


def factors_kernel(pos_ref, low_ref, mixed_ref, own_ref, send_ref):
    for ref, which in ((own_ref, pos_ref[1]), (send_ref, 1 - pos_ref[1])):
        pick = chosen_rows(which)
        ref[0] = dot(pick, low_ref[...], NT).astype(BF)
        ref[1] = dot(pick, mixed_ref[...], NT).astype(BF)


def time_forward_kernel(x_ref, wq_ref, wo_ref, middle_ref, qkv_ref, low_ref, mixed_ref):
    x = x_ref[...].astype(F32)
    normed, _ = normalize(x)
    low = normed.astype(BF)
    low_ref[...] = low
    for i in range(9):
        cols = slice(i * 256, (i + 1) * 256)
        qkv_ref[:, cols] = dot(low, wq_ref[:, cols]).astype(BF)
    keep = lanes(T)
    near = same_patch()
    for p in range(PAIRS):
        q, k, v = (qkv_ref[:, i * D + p * PAIR:i * D + (p + 1) * PAIR] for i in range(3))
        weights = []
        values = []
        for odd in (False, True):
            s = dot(keep(q, odd), k, NT)
            s = jnp.where(near, s, -1e30)
            e = jnp.exp((s - jnp.max(s, axis=1, keepdims=True)) * SCALE)
            weights.append((e / jnp.sum(e, axis=1, keepdims=True)).astype(BF))
            values.append(keep(v, odd))
        mixed = dot(jnp.concatenate(weights, axis=1), jnp.concatenate(values, axis=0))
        mixed_ref[:, p * PAIR:(p + 1) * PAIR] = mixed.astype(BF)
    middle_ref[...] = (x + dot(mixed_ref[...], wo_ref[...])).astype(BF)


def probs_back(q, k, v, g, near):
    s = dot(k, q, NT)
    if near is not None:
        s = jnp.where(near, s, -1e30)
    e = jnp.exp((s - jnp.max(s, axis=0, keepdims=True)) * SCALE)
    probs = e / jnp.sum(e, axis=0, keepdims=True)
    dprobs = dot(v, g, NT)
    delta = jnp.sum(dprobs * probs, axis=0, keepdims=True)
    return probs.astype(BF), (probs * (dprobs - delta) * SCALE).astype(BF)


def attend_back(qkv_ref, g_ref, dqkv_ref, mixed_ref, near, blocks):
    size = T // blocks
    keep = lanes(size)
    for p in range(PAIRS):
        for b in range(blocks):
            rows = slice(b * size, (b + 1) * size)
            at = [slice(i * D + p * PAIR, i * D + (p + 1) * PAIR) for i in range(3)]
            q, k, v = (qkv_ref[rows, at[i]] for i in range(3))
            g = g_ref[rows, at[0]]
            qs, ks, vs, gs, ws, ds = [], [], [], [], [], []
            for odd in (False, True):
                q1, k1, v1, g1 = (keep(a, odd) for a in (q, k, v, g))
                w, d = probs_back(q, k1, v1, g, near)
                for into, a in ((qs, q1), (ks, k1), (vs, v1), (gs, g1), (ws, w), (ds, d)):
                    into.append(a)
            qs, ks, vs, gs = (jnp.concatenate(a, axis=0) for a in (qs, ks, vs, gs))
            dqkv_ref[rows, at[1]] = dot(jnp.concatenate(ds, axis=1), qs).astype(BF)
            dqkv_ref[rows, at[2]] = dot(jnp.concatenate(ws, axis=1), gs).astype(BF)
            dqkv_ref[rows, at[0]] = dot(jnp.concatenate(ds, axis=0), ks, TN).astype(BF)
            if mixed_ref is not None:
                mixed_ref[rows, at[0]] = dot(jnp.concatenate(ws, axis=0), vs, TN).astype(BF)


def project_back_kernel(cot_ref, wo_ref, g_ref):
    g_ref[...] = dot(cot_ref[...], wo_ref[...], NT).astype(BF)


def space_kernel(m_ref, cot_ref, g_ref, wq_ref, grad_ref, dqkv_ref, x_ref, low_ref, mixed_ref, qkv_ref):
    x_ref[...] = dot(order(False), m_ref[...]).astype(BF)
    normed, inverse = normalize(x_ref[...].astype(F32))
    low = normed.astype(BF)
    low_ref[...] = low
    for i in range(9):
        cols = slice(i * 256, (i + 1) * 256)
        qkv_ref[:, cols] = dot(low, wq_ref[:, cols]).astype(BF)
    attend_back(qkv_ref, g_ref, dqkv_ref, mixed_ref, None, 2)
    grad = dot(dqkv_ref[...], wq_ref[...], NT)
    grad = cot_ref[...].astype(F32) + normalize_back(normed, inverse, grad)
    grad_ref[...] = dot(order(True), grad.astype(BF)).astype(BF)


def space_out_kernel(x_ref, mixed_ref, wo_ref, out_ref):
    out_ref[...] = (x_ref[...].astype(F32) + dot(mixed_ref[...], wo_ref[...])).astype(BF)


def turned(pos, k):
    return (pos + k) % 4


def turned(pos, k):
    return (pos + k) % 4


def time_attend_kernel(gm_ref, qkv_ref, wo_ref, dqkv_ref, g_ref):
    g_ref[...] = dot(gm_ref[...], wo_ref[...], NT).astype(BF)
    attend_back(qkv_ref, g_ref, dqkv_ref, None, same_patch(), 1)


def time_grad_kernel(x_ref, gm_ref, dqkv_ref, wq_ref, grad_ref):
    normed, inverse = normalize(x_ref[...].astype(F32))
    grad = dot(dqkv_ref[...], wq_ref[...], NT)
    grad_ref[...] = (gm_ref[...].astype(F32) + normalize_back(normed, inverse, grad)).astype(BF)


def weights_kernel(pos_ref, l_ref, l2_ref, d_ref, d2_ref, g_ref, g2_ref, o_ref):
    over_x = pos_ref[1] == 0
    for a_ref, b_ref, which, at, width in ((g_ref, g2_ref, 1, QKV, OUT), (d_ref, d2_ref, 0, 0, QKV)):
        left = jnp.concatenate([l_ref[which], l2_ref[which]], axis=1)
        part = dot(left, jnp.concatenate([a_ref[...], b_ref[...]], axis=0)).astype(BF)
        for i in range(4):
            for j in range(4):
                block = part[i * BLOCK:(i + 1) * BLOCK, j * width:(j + 1) * width]
                o_ref[jnp.where(over_x, j, i), jnp.where(over_x, i, j), :, at:at + width] = block


def weights_by_distance_kernel(pos_ref, l_ref, l2_ref, d_ref, d2_ref, g_ref, g2_ref, *refs):
    outs, held_ref = refs[:4], refs[4]
    weights_kernel(pos_ref, l_ref, l2_ref, d_ref, d2_ref, g_ref, g2_ref, held_ref)
    for k in range(4):
        outs[k][...] = held_ref[turned(pos_ref[2], k)]


def add(refs):
    total = refs[0][...].astype(F32)
    for ref in refs[1:]:
        total += ref[...].astype(F32)
    return total.astype(BF)


def add_first(ref):
    total = ref[0].astype(F32)
    for i in range(1, ref.shape[0]):
        total += ref[i].astype(F32)
    return total.astype(BF)


def sum_kernel(*refs):
    refs[4][...] = add(refs[:4])


def pieces_kernel(pos_ref, s_ref, *refs):
    for k in range(4):
        owner = turned(pos_ref[3], k)
        refs[4 + k][:, :D] = add([ref.at[owner] for ref in refs[:4]])
        refs[4 + k][:, D:] = add([s_ref.at[i, owner] for i in range(4)])


def copies_kernel(got_ref, o_ref):
    total = add_first(got_ref)
    for i in range(8):
        o_ref[i] = total


def spread_kernel(got_ref, *outs):
    for i in range(2):
        for j in range(4):
            part = add([got_ref.at[2 * j, :, i * D:(i + 1) * D], got_ref.at[2 * j + 1, :, i * D:(i + 1) * D]]).astype(F32)
            outs[2 * i][:, j * QKV:(j + 1) * QKV] = part[:, :QKV]
            outs[2 * i + 1][:, j * OUT:(j + 1) * OUT] = part[:, QKV:]


def sds(*shape, dtype=BF):
    return jax.ShapeDtypeStruct(shape, dtype)


SMEM = pl.BlockSpec(memory_space=pltpu.SMEM)
VMEM = pl.BlockSpec(memory_space=pltpu.VMEM)


def call(kernel, outs, args, flops, scratch=(), mib=48):
    moved = sum(a.size * a.dtype.itemsize for a in (*args, *outs))
    return pl.pallas_call(
        kernel,
        out_shape=outs,
        in_specs=[SMEM if a.dtype == jnp.int32 else VMEM for a in args],
        out_specs=[VMEM] * len(outs),
        scratch_shapes=scratch,
        compiler_params=pltpu.CompilerParams(vmem_limit_bytes=mib * 2**20),
        cost_estimate=pl.CostEstimate(flops=flops, bytes_accessed=moved if flops else 0, transcendentals=0),
    )(*args)


PROJ = 2 * T * D * 3 * D
OUTP = 2 * T * D * D


def permuted(x, to_sent):
    return call(functools.partial(permute_kernel, to_sent), [sds(T, D)], [x], 2 * T * T * D)[0]


def a2a(x, axes):
    return lax.all_to_all(x, axes, 0, 0, tiled=True)


def factors(pos, low, mixed):
    return call(
        factors_kernel, [sds(2, HALF, T)] * 2, [pos, low, mixed], 2 * OUTP, mib=WHOLE
    )


def weights(*factors):
    return call(weights_kernel, [sds(4, 4, BLOCK, D)], factors, 2 * 512 * HALF * 4 * D, mib=WHOLE)[0]


def rings(first):
    device = [[[(i * 4 + j) * 2 + core for core in range(2)] for j in range(4)] for i in range(4)]
    along_x = [[device[i][j][1 - first] for i in range(4)] for j in range(4)]
    along_y = [[device[i][j][first] for j in range(4)] for i in range(4)]
    return along_x + along_y


def crossed(x, first):
    return lax.all_to_all(x, ("x", "y", "c"), 0, 0, tiled=True, axis_index_groups=rings(first))


def crossed_steps(pieces, first):
    steps = {0: pieces[0]}
    for k in (2, 1, 3):
        pairs = [(ring[i], ring[(i + k) % 4]) for ring in rings(first) for i in range(4)]
        steps[k] = lax.ppermute(pieces[k], ("x", "y", "c"), pairs)
    return [steps[k] for k in (0, 2, 1, 3)]


def swap(x):
    return lax.ppermute(x, "c", [(0, 1), (1, 0)])


def after(*arrays):
    return lax.optimization_barrier(arrays)


def on_device(tokens, block_cotangent, time_qkv, time_out, space_qkv, space_out):
    x_at, y_at, core = (lax.axis_index(axis).astype(jnp.int32) for axis in ("x", "y", "c"))
    pos = jnp.stack([x_at, core, jnp.where(core == 0, x_at, y_at), jnp.where(core == 0, y_at, x_at)])
    cot = block_cotangent.reshape(T, D)
    x = a2a(permuted(tokens.reshape(T, D), True), FP)
    x, cot_other = after(x, swap(cot))
    middle, t_qkv, t_low, t_mixed = call(
        time_forward_kernel,
        [sds(T, D), sds(T, 3 * D), sds(T, D), sds(T, D)],
        [x, time_qkv, time_out],
        PROJ + OUTP, mib=WHOLE,
    )
    middle = a2a(middle, FP)
    t_own, t_send = factors(pos, t_low, t_mixed)
    s_dmixed = call(project_back_kernel, [sds(T, D)], [cot, space_out], OUTP, mib=WHOLE)[0]
    middle, t_other, s_dmixed = after(middle, swap(t_send), s_dmixed)
    grad_middle, s_dqkv, natural, s_low, s_mixed = call(
        space_kernel,
        [sds(T, D), sds(T, 3 * D), sds(T, D), sds(T, D), sds(T, D)],
        [middle, cot, s_dmixed, space_qkv],
        2 * PROJ,
        [pltpu.VMEM((T, 3 * D), BF)], mib=WHOLE,
    )
    grad_middle = a2a(grad_middle, FP)
    s_own, s_send = factors(pos, s_low, s_mixed)
    space = weights(pos, s_own, swap(s_send), s_dqkv, swap(s_dqkv), cot, cot_other)
    block_out = call(space_out_kernel, [sds(T, D)], [natural, s_mixed, space_out], OUTP, mib=WHOLE)[0]
    grad_middle, block_out, space = after(grad_middle, block_out, space)
    space = crossed(space, 1)
    t_dqkv = call(
        time_attend_kernel, [sds(T, 3 * D)], [grad_middle, t_qkv, time_out], PROJ + OUTP, [pltpu.VMEM((T, D), BF)]
    )[0]
    grad_tokens = call(time_grad_kernel, [sds(T, D)], [x, grad_middle, t_dqkv, time_qkv], PROJ)[0]
    time = call(
        weights_by_distance_kernel, [sds(4, BLOCK, D)] * 4,
        [pos, t_own, t_other, t_dqkv, swap(t_dqkv), grad_middle, swap(grad_middle)], 2 * 512 * HALF * 4 * D,
        [pltpu.VMEM((4, 4, BLOCK, D), BF)], mib=WHOLE,
    )
    grad_tokens, space, *time = after(grad_tokens, space, *time)
    tokens_grad = a2a(grad_tokens, FP)
    pieces = call(
        pieces_kernel, [sds(BLOCK, 2 * D)] * 4, [pos, space, *crossed_steps(time, 1)], 0,
    )
    got = call(sum_kernel, [sds(BLOCK, 2 * D)], crossed_steps(pieces, 0), 0)[0]
    got, tokens_grad = after(got, tokens_grad)
    got = a2a(got.reshape(4, ROWS, 2 * D), ("zh",))
    tokens_grad = permuted(tokens_grad, False)
    shares = call(copies_kernel, [sds(8, ROWS, 2 * D)], [got], 0)[0]
    sizes = [3 * D, D, 3 * D, D]
    sums = call(spread_kernel, [sds(ROWS, size, dtype=F32) for size in sizes], [a2a(shares, CLIP)], 0)
    shape = tokens.shape
    return (block_out.reshape(shape), tokens_grad.reshape(shape), *sums)


def solution(mesh):
    fine = Mesh(mesh.devices.reshape(4, 2, 4, 4, 2), ("x", "zl", "y", "zh", "c"))
    activations = P(CLIP, FP, None, None)
    return jax.shard_map(
        on_device,
        mesh=fine,
        in_specs=(activations, activations, P(), P(), P(), P()),
        out_specs=(activations, activations, P(FP, None), P(FP, None), P(FP, None), P(FP, None)),
        check_vma=False,
    )
```
